32 devices in a mesh: dp: 8 (over z, y), tensor: 4 (over x, core).
Axes of the slice: x: 2, y: 2, z: 4, core: 2. Of those that a mesh axis runs over, the one named last changes fastest.
Arguments:
- hidden: bfloat16 [1024, 3072], P('dp', 'tensor'), may hold values from -6 to 6
- cotangent: bfloat16 [1024, 4096], P('dp', 'tensor'), may hold values from -6 to 6
- blocks: bfloat16 [256, 128, 128], P('tensor'), may hold values from -0.1875 to 0.1875
- block_pos: int32 [4, 64], P('tensor'), may hold values from 0 to 191, as said below
- owner_rank: int32 [4, 64], P('tensor'), may hold values from 0 to 63, each once within a row
- moment: float32 [4, 64, 128, 128], P('tensor', 'dp'), may hold values from -0.028125 to 0.028125
- second: float32 [4, 64, 128, 128], P('tensor', 'dp'), may hold values from 2.4414062e-06 to 3.90625e-05
Outputs:
- mixed: bfloat16 [1024, 4096], P('dp', 'tensor')
- hidden_grad: bfloat16 [1024, 3072], P('dp', 'tensor')
- new_moment: float32 [4, 64, 128, 128], P('tensor', 'dp')
- new_second: float32 [4, 64, 128, 128], P('tensor', 'dp')
- direction: float32 [4, 64, 128, 128], P('tensor', 'dp')
- new_blocks: bfloat16 [256, 128, 128], P('tensor')
The draws below stay inside these ranges and needn't reach their ends.
Inputs may be any that keep to these rules, and one draw needn't show every extreme that they name: `block_pos`: each row holds 64 different positions of the 6 x 32 blocks of one slab, in no order. `owner_rank`: the block of rank k has its optimizer state at dp index k // 8.
All inputs are finite; a program needn't handle non-finite values.
Results may differ from the reference program's by a relative error of at most 0.017.
Values may be sent and summed in bfloat16 or wider, within the bound.
A program may use at most 64 MiB of HBM per device.

```python
import math
import jax
import jax.numpy as jnp
from jax import lax

D = 4096
FF_DEV = 768
BS = 128
SLOTS = 64
FF = 3072
TOKENS = 1024
N_TENSOR = 4


def draw_block_pos(key, part):
    row_keys = jax.random.split(jax.random.fold_in(key, 7), N_TENSOR)

    def one_row(row_key):
        return jax.random.permutation(row_key, FF_DEV // BS * (D // BS))[:SLOTS]
    return jax.vmap(one_row)(row_keys).astype(jnp.int32)


def steps_of(rng, dims, cuts, low, largest):
    gain, own = 1.0, jax.random.fold_in(rng, 6)
    for dim, parts in cuts:
        draws = jnp.exp(jax.random.uniform(jax.random.fold_in(own, dim), (parts,), jnp.float32, low / len(cuts), largest / len(cuts)))
        gain = gain * jnp.repeat(draws, dims[dim] // parts).reshape([-1 if axis == dim else 1 for axis in range(len(dims))])
    return gain


def bell_draw(key, extent, spread, reach, shards=(), kind=jnp.bfloat16):
    array = spread * jax.random.normal(key, extent, jnp.float32)
    if shards:
        array = array * steps_of(key, extent, shards, -0.22, 0.18)
    return jnp.clip(array, -reach, reach).astype(kind)


def setup_inputs(seed: int = 0) -> dict:
    arg_keys = jax.random.split(jax.random.key(seed), 8)
    hidden = bell_draw(arg_keys[0], (TOKENS, FF), 1.0, 6.0, ((0, 8), (1, 4)))
    cotangent = bell_draw(arg_keys[1], (TOKENS, D), 1.0, 6.0, ((0, 8), (1, 4)))
    blocks = bell_draw(arg_keys[2], (N_TENSOR * SLOTS, BS, BS), (BS * SLOTS * N_TENSOR // (D // BS)) ** -0.5, 0.1875, ((0, 4),))
    block_pos = draw_block_pos(jax.random.fold_in(arg_keys[7], 71), 0)
    owner_rank = jax.vmap(lambda own: jax.random.permutation(own, SLOTS))(jax.random.split(arg_keys[4], N_TENSOR)).reshape((N_TENSOR, SLOTS)).astype(jnp.int32)
    moment = bell_draw(arg_keys[5], (N_TENSOR, SLOTS, BS, BS), (0.15 * TOKENS ** -0.5), 0.028125, ((0, 4), (1, 8)), jnp.float32)
    second = jnp.clip(jnp.exp(math.log(3.9062499126885086e-05) - 2.7725887 * jax.random.uniform(arg_keys[6], (N_TENSOR, SLOTS, BS, BS), jnp.float32) ** steps_of(arg_keys[6], (N_TENSOR, SLOTS, BS, BS), ((0, 4), (1, 8)), -0.2, 0.2)), 2.441406195430318e-06, 3.9062499126885086e-05)
    return dict(hidden=hidden, cotangent=cotangent, blocks=blocks, block_pos=block_pos, owner_rank=owner_rank, moment=moment, second=second)


def reference(hidden, cotangent, blocks, block_pos, owner_rank, moment, second):
    fblk = FF_DEV // BS
    dblk = D // BS
    hid_slabs = hidden.reshape(TOKENS, N_TENSOR, fblk, BS).transpose(1, 0, 2, 3)
    grad_blocks = cotangent.reshape(TOKENS, dblk, BS).astype(jnp.float32)
    slab_blocks = blocks.reshape(N_TENSOR, SLOTS, BS, BS)
    highest = lax.Precision.HIGHEST

    def one_slab(carry, inputs):
        hid_t, blk_t, pos_t, rank_t, mom_t, sec_t = inputs
        block_rows = (pos_t // dblk).astype(jnp.int32)
        block_cols = (pos_t % dblk).astype(jnp.int32)
        chosen_hid = jnp.take(hid_t, block_rows, axis=1).astype(jnp.float32)
        chosen_grad = jnp.take(grad_blocks, block_cols, axis=1)
        weights = blk_t.astype(jnp.float32)
        col_hot = (block_cols[:, None] == jnp.arange(dblk)[None, :]).astype(jnp.float32)
        row_hot = (block_rows[:, None] == jnp.arange(fblk)[None, :]).astype(jnp.float32)
        contrib = jnp.einsum('nsa,sab->nsb', chosen_hid, weights, precision=highest)
        partial_value = jnp.einsum('nsb,sc->ncb', contrib, col_hot, precision=highest).reshape(TOKENS, D)
        partial_value = lax.optimization_barrier(partial_value.astype(jnp.bfloat16)).astype(jnp.float32)
        back = jnp.einsum('nsb,sab->nsa', chosen_grad, weights, precision=highest)
        hid_grad = jnp.einsum('nsa,sr->nra', back, row_hot, precision=highest).reshape(TOKENS, FF_DEV).astype(jnp.bfloat16)
        grads = jnp.einsum('nsa,nsb->sab', chosen_hid, chosen_grad, precision=highest) * (1.0 / TOKENS)
        order = jnp.argsort(rank_t).astype(jnp.int32)
        grads_ranked = jnp.take(grads, order, axis=0)
        weights_ranked = jnp.take(weights, order, axis=0)
        mom_next = 0.9 * mom_t + 0.1 * grads_ranked
        sec_next = 0.999 * sec_t + 0.001 * grads_ranked * grads_ranked
        step_dir = mom_next / (jnp.sqrt(sec_next) + 1e-08)
        updated = (weights_ranked - 0.002 * (step_dir + 0.1 * weights_ranked)).astype(jnp.bfloat16)
        listed = jnp.take(updated, rank_t.astype(jnp.int32), axis=0)
        return (carry + partial_value, (hid_grad, mom_next, sec_next, step_dir, listed))
    start = jnp.zeros((TOKENS, D), jnp.float32)
    total, outs = lax.scan(one_slab, start, (hid_slabs, slab_blocks, block_pos, owner_rank, moment, second))
    hid_grads, new_moment, new_second, direction, listed = outs
    mixed = total.astype(jnp.bfloat16)
    hidden_grad = hid_grads.transpose(1, 0, 2).reshape(TOKENS, N_TENSOR * FF_DEV)
    new_blocks = listed.reshape(N_TENSOR * SLOTS, BS, BS)
    return (mixed, hidden_grad, new_moment, new_second, direction, new_blocks)
```

```python
import functools

import jax
import jax.numpy as jnp
from jax import lax
from jax.experimental import pallas as pl
from jax.experimental.pallas import tpu as pltpu
from jax.sharding import PartitionSpec as P

CORES = 2
MESH = pl.DeviceIdType.MESH
F32 = jnp.float32
BF16 = jnp.bfloat16


def split_dp(dp):
    wide = 1
    while (wide * 2) ** 2 <= dp and dp % (wide * 2) == 0:
        wide *= 2
    return dp // wide, wide


def step_kernel(
    dims, hid, ct, blk, table, rank, mom, sec,
    mixed_o, hgrad_o, nm_o, ns_o, nd_o, nb_o,
    hid_all, hid_t, ct_all, ct_col, blk_v, dense, part_s, part_r, mixed_v, hgrad_v,
    grad_s, from_lo, from_hi, mom_v, sec_v, dir_v, gathered, listed,
    hid_r, ct_r, part_rs, lo_r, hi_r, ag_r,
    hid_ss, ct_ss, fwd_ss, core_ss, part_ss, rs_ss, agz_ss, agd_ss, agy_ss,
    loc, out_s,
):
    dp, tn = dims
    lines, wide = split_dp(dp)
    cores = CORES if tn % CORES == 0 else 1
    chips = tn // cores
    n, ff = hid.shape
    cw = ct.shape[1]
    width = cw * tn
    slots, bs = blk.shape[0], blk.shape[1]
    cols = width // bs
    row_blocks = ff // bs
    owned = mom.shape[0]
    chunks = grad_s.shape[1]
    cb = owned // chunks

    d = lax.axis_index("dp")
    t = lax.axis_index("tensor")
    z, y = d // wide, d % wide
    x, core = t // cores, t % cores

    def ys(i):
        return (y + i) % wide

    def xs(j):
        return ((x + j) % chips) * cores + core

    mate = x * cores + (core + 1) % cores

    barrier = pltpu.get_barrier_semaphore()
    for i in range(1, tn):
        pl.semaphore_signal(barrier, inc=1, device_id={"tensor": (t + i) % tn}, device_id_type=MESH)
    for i in range(1, wide):
        pl.semaphore_signal(barrier, inc=1, device_id={"dp": z * wide + ys(i)}, device_id_type=MESH)

    @pl.when(z > 0)
    def _():
        pl.semaphore_signal(barrier, inc=1, device_id={"dp": d - wide}, device_id_type=MESH)

    @pl.when(z < lines - 1)
    def _():
        pl.semaphore_signal(barrier, inc=1, device_id={"dp": d + wide}, device_id_type=MESH)

    my_rows = pl.ds(pl.multiple_of(y * n, n), n)
    my_cols = pl.ds(pl.multiple_of(t * cw, cw), cw)
    load_hid = pltpu.make_async_copy(hid, hid_all.at[my_rows, :], loc.at[0])
    load_ct = pltpu.make_async_copy(ct, ct_all.at[my_rows, my_cols], loc.at[1])
    load_blk = pltpu.make_async_copy(blk, blk_v.at[pl.ds(0, slots)], loc.at[2])
    load_mom = pltpu.make_async_copy(mom, mom_v, loc.at[3])
    load_sec = pltpu.make_async_copy(sec, sec_v, loc.at[4])
    for copy in (load_hid, load_blk, load_ct, load_mom, load_sec):
        copy.start()

    near = jnp.where(z > 0, 1, 0) + jnp.where(z < lines - 1, 1, 0)
    pl.semaphore_wait(barrier, tn - 1 + wide - 1 + near)

    def ct_slot(yy, tt):
        return ct_all.at[
            pl.ds(pl.multiple_of(yy * n, n), n), pl.ds(pl.multiple_of(tt * cw, cw), cw)
        ]

    def ct_copy(src, yy, tt, send, device):
        return pltpu.make_async_remote_copy(
            src_ref=src, dst_ref=ct_slot(yy, tt), send_sem=send,
            recv_sem=ct_r.at[yy * tn + tt], device_id=device, device_id_type=MESH,
        )

    def ct_arrival(yy, tt):
        ct_copy(ct_slot(yy, tt), yy, tt, ct_ss.at[0], {"tensor": mate}).wait_recv()

    sent = []

    def launch(copy):
        copy.start()
        sent.append(copy)

    for i in range(1, wide):
        launch(ct_copy(ct, y, t, ct_ss.at[i - 1], {"dp": z * wide + ys(i)}))
    for j in range(1, chips):
        launch(ct_copy(ct, y, t, ct_ss.at[wide - 1 + j - 1], {"tensor": xs(j)}))
    if cores > 1:
        launch(ct_copy(ct, y, t, ct_ss.at[wide + chips - 2], {"tensor": mate}))
    for i in range(1, wide):
        launch(pltpu.make_async_remote_copy(
            src_ref=hid, dst_ref=hid_all.at[my_rows, :], send_sem=hid_ss.at[i - 1],
            recv_sem=hid_r.at[y], device_id={"dp": z * wide + ys(i)}, device_id_type=MESH,
        ))

    blk_v[slots] = jnp.zeros((bs, bs), BF16)
    load_blk.wait()
    lanes = table.shape[1]

    def place(c, carry):
        for r in range(row_blocks):
            p = r * cols + c
            s = table[3 + p // lanes, p % lanes]
            dense[pl.ds(r * bs, bs), pl.ds(pl.multiple_of(c * bs, bs), bs)] = blk_v[s]
        return carry

    lax.fori_loop(0, cols, place, 0)
    load_hid.wait()
    tile = min(256, cw)

    def forward(k, carry):
        tt, c = k // (cw // tile), k % (cw // tile)
        value = jnp.dot(
            hid_all[my_rows, :],
            dense[:, pl.ds(pl.multiple_of(k * tile, tile), tile)],
            preferred_element_type=F32,
        )
        part_s[tt, :, pl.ds(pl.multiple_of(c * tile, tile), tile)] = value.astype(BF16)
        return carry

    lax.fori_loop(0, width // tile, forward, 0)

    load_ct.wait()
    for i in range(1, wide):
        yy = ys(i)
        ct_arrival(yy, t)
        for j in range(1, chips):
            launch(ct_copy(
                ct_slot(yy, t), yy, t, fwd_ss.at[(i - 1) * (chips - 1) + j - 1],
                {"tensor": xs(j)},
            ))
        if cores > 1:
            launch(ct_copy(ct_slot(yy, t), yy, t, core_ss.at[i - 1], {"tensor": mate}))
    for j in range(1, chips):
        ct_arrival(y, xs(j))
        if cores > 1:
            launch(ct_copy(
                ct_slot(y, xs(j)), y, xs(j), core_ss.at[wide - 1 + j - 1], {"tensor": mate}
            ))
    if cores > 1:
        for j in range(chips):
            ct_arrival(y, ((x + j) % chips) * cores + (core + 1) % cores)

    rtile = 256 if ff % 256 == 0 else bs

    def backward(k, carry):
        rows = pl.ds(pl.multiple_of(k * rtile, rtile), rtile)
        value = lax.dot_general(
            ct_all[my_rows, :], dense[rows, :], (((1,), (1,)), ((), ())),
            preferred_element_type=F32,
        )
        hgrad_v[:, rows] = value.astype(BF16)
        return carry

    lax.fori_loop(0, ff // rtile, backward, 0)
    store_hgrad = pltpu.make_async_copy(hgrad_v, hgrad_o, out_s.at[0])
    store_hgrad.start()

    for i in range(1, wide):
        yy = ys(i)
        pltpu.make_async_remote_copy(
            src_ref=hid, dst_ref=hid_all.at[pl.ds(pl.multiple_of(yy * n, n), n), :],
            send_sem=hid_ss.at[0], recv_sem=hid_r.at[yy],
            device_id={"tensor": mate}, device_id_type=MESH,
        ).wait_recv()

    def flip(k, carry):
        rows = pl.ds(pl.multiple_of(k * bs, bs), bs)
        hid_t[k] = hid_all[:, rows].T
        return carry

    lax.fori_loop(0, row_blocks, flip, 0)

    for i in range(1, wide):
        for j in range(1, chips):
            yy = ys(i)
            ct_arrival(yy, xs(j))
            if cores > 1:
                launch(ct_copy(
                    ct_slot(yy, xs(j)), yy, xs(j),
                    core_ss.at[wide + chips - 2 + (i - 1) * (chips - 1) + j - 1],
                    {"tensor": mate},
                ))
    if cores > 1:
        for i in range(1, wide):
            for j in range(chips):
                ct_arrival(ys(i), ((x + j) % chips) * cores + (core + 1) % cores)

    def by_column(k, carry):
        ct_col[k] = ct_all[:, pl.ds(pl.multiple_of(k * bs, bs), bs)]
        return carry

    lax.fori_loop(0, cols, by_column, 0)

    for i in range(1, tn):
        peer = (t + i) % tn
        launch(pltpu.make_async_remote_copy(
            src_ref=part_s.at[peer], dst_ref=part_r.at[t], send_sem=part_ss.at[i - 1],
            recv_sem=part_rs.at[t], device_id={"tensor": peer}, device_id_type=MESH,
        ))

    def own_grad(owner, c, k):
        r = (owner * wide + y) * owned + c * cb + k
        return jnp.dot(hid_t[table[1, r]], ct_col[table[2, r]], preferred_element_type=F32)

    def sum_copy(owner, c, up):
        into, sems = (from_lo, lo_r) if up else (from_hi, hi_r)
        return pltpu.make_async_remote_copy(
            src_ref=grad_s.at[owner, c], dst_ref=into.at[owner, c],
            send_sem=rs_ss.at[owner * chunks + c], recv_sem=sems.at[owner * chunks + c],
            device_id={"dp": d + wide if up else d - wide}, device_id_type=MESH,
        )

    def pass_sum(owner, c, up):
        inner = (z > 0) if up else (z < lines - 1)
        into = from_lo if up else from_hi

        @pl.when(inner)
        def _():
            sum_copy(owner, c, up).wait_recv()
            for k in range(cb):
                value = own_grad(owner, c, k) + into[owner, c, k].astype(F32)
                grad_s[owner, c, k] = value.astype(BF16)

        @pl.when(jnp.logical_not(inner))
        def _():
            for k in range(cb):
                grad_s[owner, c, k] = own_grad(owner, c, k).astype(BF16)

        sum_copy(owner, c, up).start()

    def pass_sums(c):
        for dist in range(lines - 1, 0, -1):
            @pl.when(z + dist < lines)
            def _():
                pass_sum(z + dist, c, True)

            @pl.when(z - dist >= 0)
            def _():
                pass_sum(z - dist, c, False)

    def new_copy(owner, yy, c, send, device):
        slot = gathered.at[pl.ds((owner * wide + yy) * owned + c * cb, cb)]
        return pltpu.make_async_remote_copy(
            src_ref=slot, dst_ref=slot, send_sem=send,
            recv_sem=ag_r.at[(owner * wide + yy) * chunks + c],
            device_id=device, device_id_type=MESH,
        )

    def new_up(owner, c):
        return new_copy(owner, y, c, agz_ss.at[owner * chunks + c], {"dp": d + wide})

    def new_down(owner, c):
        sem = agd_ss.at[owner * chunks + c]
        return new_copy(owner, y, c, sem, {"dp": d - wide})

    def new_side(owner, c, i):
        sem = agy_ss.at[(owner * chunks + c) * (wide - 1) + i - 1]
        return new_copy(owner, y, c, sem, {"dp": z * wide + ys(i)})

    factor = 1.0 / (n * dp)

    def finish(c):
        for low in (True, False):
            @pl.when((z > 0) if low else (z < lines - 1))
            def _():
                sum_copy(z, c, low).wait_recv()
        lo_on = jnp.where(z > 0, 1, 0)
        hi_on = jnp.where(z < lines - 1, 1, 0)
        for k in range(cb):
            at = c * cb + k
            dir_v[at] = own_grad(z, c, k)

            @pl.when(lo_on == 1)
            def _():
                dir_v[at] += from_lo[z, c, k].astype(F32)

            @pl.when(hi_on == 1)
            def _():
                dir_v[at] += from_hi[z, c, k].astype(F32)

            g = dir_v[at] * factor
            m = 0.9 * mom_v[at] + 0.1 * g
            v = 0.999 * sec_v[at] + 0.001 * g * g
            step = m / (jnp.sqrt(v) + 1e-08)
            mom_v[at] = m
            sec_v[at] = v
            dir_v[at] = step
            w = blk_v[table[0, d * owned + at]].astype(F32)
            gathered[d * owned + at] = (w - 0.002 * (step + 0.1 * w)).astype(BF16)

        @pl.when(z < lines - 1)
        def _():
            new_up(z, c).start()

        @pl.when(z > 0)
        def _():
            new_down(z, c).start()

        for i in range(1, wide):
            new_side(z, c, i).start()

    def pass_new(c):
        for dist in range(1, lines):
            @pl.when(z - dist >= 0)
            def _():
                new_up(z - dist, c).wait_recv()

                @pl.when(z < lines - 1)
                def _():
                    new_up(z - dist, c).start()

                for i in range(1, wide):
                    new_side(z - dist, c, i).start()

            @pl.when(z + dist < lines)
            def _():
                new_down(z + dist, c).wait_recv()

                @pl.when(z > 0)
                def _():
                    new_down(z + dist, c).start()

                for i in range(1, wide):
                    new_side(z + dist, c, i).start()

    load_mom.wait()
    load_sec.wait()
    pass_sums(0)
    for c in range(chunks):
        finish(c)
        if c + 1 < chunks:
            pass_sums(c + 1)
        if c > 0:
            pass_new(c - 1)
    store_nm = pltpu.make_async_copy(mom_v, nm_o, out_s.at[1])
    store_ns = pltpu.make_async_copy(sec_v, ns_o, out_s.at[2])
    store_nd = pltpu.make_async_copy(dir_v, nd_o, out_s.at[3])
    for copy in (store_nm, store_ns, store_nd):
        copy.start()

    for i in range(1, tn):
        peer = (t + i) % tn
        pltpu.make_async_remote_copy(
            src_ref=part_s.at[peer], dst_ref=part_r.at[peer], send_sem=part_ss.at[i - 1],
            recv_sem=part_rs.at[peer], device_id={"tensor": peer}, device_id_type=MESH,
        ).wait_recv()

    def add_parts(k, carry):
        at = pl.ds(pl.multiple_of(k * bs, bs), bs)
        value = part_s[t, :, at].astype(F32)
        for i in range(1, tn):
            value = value + part_r[(t + i) % tn, :, at].astype(F32)
        mixed_v[:, at] = value.astype(BF16)
        return carry

    lax.fori_loop(0, cw // bs, add_parts, 0)
    store_mixed = pltpu.make_async_copy(mixed_v, mixed_o, out_s.at[4])
    store_mixed.start()

    pass_new(chunks - 1)
    for c in range(chunks):
        for owner in range(lines):
            for i in range(1, wide):
                new_copy(owner, ys(i), c, agy_ss.at[0], {"tensor": mate}).wait_recv()

    def relist(s, carry):
        listed[s] = gathered[rank[0, s]]
        return carry

    lax.fori_loop(0, slots, relist, 0, unroll=8)
    store_nb = pltpu.make_async_copy(listed, nb_o, out_s.at[5])
    store_nb.start()

    for copy in sent:
        copy.wait_send()
    for c in range(chunks):
        for owner in range(lines):
            @pl.when(owner != z)
            def _():
                sum_copy(owner, c, True).wait_send()

            @pl.when((owner <= z) & (z < lines - 1))
            def _():
                new_up(owner, c).wait_send()

            @pl.when((owner >= z) & (z > 0))
            def _():
                new_down(owner, c).wait_send()

            for i in range(1, wide):
                new_side(owner, c, i).wait_send()
    for copy in (store_hgrad, store_nm, store_ns, store_nd, store_mixed, store_nb):
        copy.wait()


def tables(pos, rank, row_blocks, cols):
    slots = pos.shape[0]
    lanes = max(128, -(-slots // 128) * 128)
    rows = -(-(3 + -(-row_blocks * cols // lanes)) // 8) * 8
    flat = jnp.arange(rows * lanes, dtype=jnp.int32)[:, None]
    part = flat // lanes
    slot = jnp.arange(slots, dtype=jnp.int32)[None, :]
    pos, rank = pos[None, :], rank[None, :]
    key = jnp.where(part < 3, rank + part * lanes, pos + 3 * lanes)
    by_rank = jnp.where(part == 0, slot, jnp.where(part == 1, pos // cols, pos % cols))
    value = jnp.where(part < 3, by_rank, slot - slots)
    found = jnp.sum(jnp.where(key == flat, value, 0), axis=1, dtype=jnp.int32)
    return jnp.where(part[:, 0] < 3, found, found + slots).reshape(rows, lanes)


def shards(dims, hidden, cotangent, blocks, block_pos, owner_rank, moment, second):
    dp, tn = dims
    lines, wide = split_dp(dp)
    chips = max(tn // CORES, 1)
    n, ff = hidden.shape
    cw = cotangent.shape[1]
    width = cw * tn
    slots, bs, _ = blocks.shape
    owned = moment.shape[1]
    chunks = 2 if owned % 2 == 0 else 1
    cb = owned // chunks
    table = tables(block_pos[0], owner_rank[0], ff // bs, width // bs)
    own_shape = moment.shape[1:]
    any_spec = pl.BlockSpec(memory_space=pl.ANY)
    smem_spec = pl.BlockSpec(memory_space=pltpu.SMEM)
    dma = pltpu.SemaphoreType.DMA

    def some(count):
        return dma((max(count, 1),))

    flops = 2 * n * width * ff * 2 + 2 * n * wide * slots * bs * bs
    out = pl.pallas_call(
        functools.partial(step_kernel, dims),
        out_shape=(
            jax.ShapeDtypeStruct((n, cw), BF16),
            jax.ShapeDtypeStruct((n, ff), BF16),
            jax.ShapeDtypeStruct(own_shape, F32),
            jax.ShapeDtypeStruct(own_shape, F32),
            jax.ShapeDtypeStruct(own_shape, F32),
            jax.ShapeDtypeStruct(blocks.shape, BF16),
        ),
        in_specs=[any_spec, any_spec, any_spec, smem_spec, smem_spec, any_spec, any_spec],
        out_specs=(any_spec,) * 6,
        scratch_shapes=[
            pltpu.VMEM((wide * n, ff), BF16),
            pltpu.VMEM((ff // bs, bs, wide * n), BF16),
            pltpu.VMEM((wide * n, width), BF16),
            pltpu.VMEM((width // bs, wide * n, bs), BF16),
            pltpu.VMEM((slots + 1, bs, bs), BF16),
            pltpu.VMEM((ff, width), BF16),
            pltpu.VMEM((tn, n, cw), BF16),
            pltpu.VMEM((tn, n, cw), BF16),
            pltpu.VMEM((n, cw), BF16),
            pltpu.VMEM((n, ff), BF16),
            pltpu.VMEM((lines, chunks, cb, bs, bs), BF16),
            pltpu.VMEM((lines, chunks, cb, bs, bs), BF16),
            pltpu.VMEM((lines, chunks, cb, bs, bs), BF16),
            pltpu.VMEM(own_shape, F32),
            pltpu.VMEM(own_shape, F32),
            pltpu.VMEM(own_shape, F32),
            pltpu.VMEM((slots, bs, bs), BF16),
            pltpu.VMEM((slots, bs, bs), BF16),
            some(wide),
            some(wide * tn),
            some(tn),
            some(lines * chunks),
            some(lines * chunks),
            some(dp * chunks),
            some(wide - 1),
            some(wide + chips - 1),
            some((wide - 1) * (chips - 1)),
            some(wide + chips - 2 + (wide - 1) * (chips - 1)),
            some(tn - 1),
            some(lines * chunks),
            some(lines * chunks),
            some(lines * chunks),
            some(lines * chunks * (wide - 1)),
            dma((6,)),
            dma((6,)),
        ],
        compiler_params=pltpu.CompilerParams(
            collective_id=0, has_side_effects=True, vmem_limit_bytes=56 * 1024 * 1024
        ),
        cost_estimate=pl.CostEstimate(
            flops=flops, bytes_accessed=16 * 1024 * 1024, transcendentals=0
        ),
        name="train_step",
    )(hidden, cotangent, blocks, table, owner_rank, moment[0], second[0])
    mixed, hidden_grad, new_moment, new_second, direction, new_blocks = out
    return (
        mixed, hidden_grad, new_moment[None], new_second[None], direction[None], new_blocks
    )


def solution(mesh):
    placed = (
        P("dp", "tensor"),
        P("dp", "tensor"),
        P("tensor", None, None),
        P("tensor", None),
        P("tensor", None),
        P("tensor", "dp", None, None),
        P("tensor", "dp", None, None),
    )
    return jax.shard_map(
        functools.partial(shards, (mesh.shape["dp"], mesh.shape["tensor"])),
        mesh=mesh,
        in_specs=placed,
        out_specs=(
            P("dp", "tensor"),
            P("dp", "tensor"),
            P("tensor", "dp", None, None),
            P("tensor", "dp", None, None),
            P("tensor", "dp", None, None),
            P("tensor", None, None),
        ),
        check_vma=False,
    )
```
